128 devices in a mesh: frame: 16 (over y, x_hi, core), patch: 8 (over z, x_lo).
Axes of the slice: x: 4 (x_hi: 2, x_lo: 2; x = x_hi * 2 + x_lo), y: 4, z: 4, core: 2. Of those that a mesh axis runs over, the one named last changes fastest.
Arguments:
- queries: bfloat16 [32, 2048, 5120], P('frame', 'patch'), may hold values from -6 to 6
- keys: bfloat16 [32, 2048, 5120], P('frame', 'patch'), may hold values from -6 to 6
- values: bfloat16 [32, 2048, 5120], P('frame', 'patch'), may hold values from -6 to 6
- spatial_mask: int32 [32, 28, 16, 16], replicated, may hold values from 0 to 1, as said below
- temporal_mask: int32 [64, 12, 8, 8], replicated, may hold values from 0 to 1, as said below
Outputs:
- attended: bfloat16 [32, 2048, 5120], P('frame', 'patch')
The draws below stay inside these ranges and needn't reach their ends.
Inputs may be any that keep to these rules, and one draw needn't show every extreme that they name: `spatial_mask`: entries are 0 or 1; every diagonal block is 1. `temporal_mask`: entries are 0 or 1; every diagonal block is 1.
All inputs are finite; a program needn't handle non-finite values.
Results may differ from the reference program's by a relative error of at most 0.0046.
Values may be sent and summed in bfloat16 or wider, within the bound.
A program may use at most 320 MiB of HBM per device.

```python
import jax
import jax.numpy as jnp
from jax import lax

HD = 128
SH = 28
TH = 12
D = 5120
GP = 32
BLOCK = 128
F = 32
P_SIZE = 2048
PB = 16
G = 64
FB = 8


def base_rows(key, salt):
    return jnp.clip(jax.random.normal(jax.random.fold_in(key, salt), (F, P_SIZE, D), jnp.float32), -6.0, 6.0)


def draw_queries(key, part):
    rows = base_rows(key, 1)
    return rows.astype(jnp.bfloat16)


def draw_keys(key, part):
    rows = base_rows(key, 2)
    return rows.astype(jnp.bfloat16)


def block_mask(key, outer, heads, count, salt):
    level = jax.random.randint(jax.random.fold_in(key, salt), (outer, heads, 1, 1), 1, 9)
    coins = jax.random.randint(jax.random.fold_in(key, salt + 1), (outer, heads, count, count), 0, 8)
    diagonal = jnp.arange(count)[:, None] == jnp.arange(count)[None, :]
    return jnp.where((coins < level) | diagonal, 1, 0).astype(jnp.int32)


def draw_spatial_mask(key, part):
    return block_mask(key, F, SH, PB, 5)


def draw_temporal_mask(key, part):
    return block_mask(key, G, TH, FB, 7)


def block_levels(rng, shape, cuts, smallest, high):
    gain, own = 1.0, jax.random.fold_in(rng, 6)
    for dim, blocks in cuts:
        heights = jnp.exp(jax.random.uniform(jax.random.fold_in(own, dim), (blocks,), jnp.float32, smallest / len(cuts), high / len(cuts)))
        gain = gain * jnp.repeat(heights, shape[dim] // blocks).reshape([-1 if axis == dim else 1 for axis in range(len(shape))])
    return gain


def normal_values(rng, dims, scale, bound, cuts=(), held_as=jnp.bfloat16):
    drawn = jax.random.normal(rng, dims, jnp.float32) * scale
    if len(cuts) > 0:
        drawn = block_levels(rng, dims, cuts, -0.22, 0.18) * drawn
    return jnp.clip(drawn, min=-bound, max=bound).astype(held_as)


def setup_inputs(seed: int = 0) -> dict:
    splits = jax.random.split(jax.random.key(seed), 6)
    return {
        "queries": draw_queries(jax.random.fold_in(splits[5], 71), 0),
        "keys": draw_keys(jax.random.fold_in(splits[5], 71), 0),
        "values": normal_values(splits[2], (F, P_SIZE, D), 1.0, 6.0, ((0, 16), (1, 8))),
        "spatial_mask": draw_spatial_mask(jax.random.fold_in(splits[5], 71), 0),
        "temporal_mask": draw_temporal_mask(jax.random.fold_in(splits[5], 71), 0),
    }


def attend(query, key_rows, value_rows, blocks):
    allowed = jnp.repeat(jnp.repeat(blocks > 0, BLOCK, axis=1), BLOCK, axis=2)
    scores = jnp.einsum("hqe,hke->hqk", query.astype(jnp.float32), key_rows.astype(jnp.float32)) * (HD ** -0.5)
    scores = jnp.where(allowed, scores, -jnp.inf)
    top = jnp.max(scores, axis=2, keepdims=True)
    probs = jnp.exp(scores - top)
    total = jnp.sum(probs, axis=2, keepdims=True)
    weights = lax.optimization_barrier(probs.astype(jnp.bfloat16))
    mixed = jnp.einsum("hqk,hke->hqe", weights.astype(jnp.float32), value_rows.astype(jnp.float32))
    return (mixed / total).astype(jnp.bfloat16)


def reference(queries, keys, values, spatial_mask, temporal_mask):
    split = SH * HD

    def spatial_frame(operands):
        query, key_rows, value_rows, blocks = operands

        def heads(rows):
            return rows[:, :split].reshape(P_SIZE, SH, HD).transpose(1, 0, 2)

        def one_head(inner):
            return attend(inner[0][None], inner[1][None], inner[2][None], inner[3][None])[0]

        mixed = lax.map(one_head, (heads(query), heads(key_rows), heads(value_rows), blocks))
        return mixed.transpose(1, 0, 2).reshape(P_SIZE, split)

    spatial_out = lax.map(spatial_frame, (queries, keys, values, spatial_mask))

    def regroup(rows):
        shaped = rows[:, :, split:].reshape(F, G, GP, TH, HD).transpose(1, 3, 0, 2, 4)
        return shaped.reshape(G, TH, F * GP, HD)

    def temporal_group(operands):
        query, key_rows, value_rows, blocks = operands
        return attend(query, key_rows, value_rows, blocks)

    grouped = lax.map(temporal_group, (regroup(queries), regroup(keys), regroup(values), temporal_mask))
    temporal_out = grouped.reshape(G, TH, F, GP, HD).transpose(2, 0, 3, 1, 4).reshape(F, P_SIZE, TH * HD)
    return jnp.concatenate([spatial_out, temporal_out], axis=2)
```

```python
import functools
import math

import jax
import jax.numpy as jnp
from jax import lax
from jax.experimental import pallas as pl
from jax.experimental.pallas import tpu as pltpu
from jax.sharding import PartitionSpec as P

HD = 128
SH = 28
TH = 12
GP = 32
BLOCK = 128
NF = 16
NP = 8
FD = 2
CELLS = 256
SEQ_S = NP * CELLS
SEQ_T = NF * FD * GP
NB_S = SEQ_S // BLOCK
NB_T = SEQ_T // BLOCK
ITEMS_S = FD * SH // NP
ITEMS_T = (CELLS // GP) * TH // NF
CHUNK = 2
CHUNKS = ITEMS_T // CHUNK
CW = CHUNK * HD
STAGES = ITEMS_S + CHUNKS
AHEAD = 3
TQ = 256
KC = 256
UNITS = 1.0 / math.sqrt(HD) * math.log2(math.e)
BIG = 1e30
MESH = pl.DeviceIdType.MESH


def attend(get_query, get_key, get_value, get_mask, put, first, length, scores_ref, value_ref):
    tiles = length // TQ
    halves = TQ // BLOCK
    for c in range(length // KC):
        value_ref[0:HD, c * KC : (c + 1) * KC] = get_value(c * KC, KC).T

    def step(d):
        tile = lax.rem(first + d, tiles)
        start = pl.multiple_of(tile * TQ, TQ)
        scaled = get_query(start, TQ).astype(jnp.float32) * UNITS
        high = scaled.astype(jnp.bfloat16)
        low = (scaled - high.astype(jnp.float32)).astype(jnp.bfloat16)
        query = jnp.concatenate([high, low], axis=1)

        def choose(j, rows, otherwise):
            parts = [
                jnp.where(
                    get_mask(tile * halves + i, j) > 0,
                    rows[:, i * BLOCK : (i + 1) * BLOCK],
                    otherwise,
                )
                for i in range(halves)
            ]
            return jnp.concatenate(parts, axis=1)

        top = jnp.full((8, TQ), -BIG, jnp.float32)
        for c in range(length // KC):
            key = get_key(c * KC, KC)
            scores = lax.dot_general(
                jnp.concatenate([key, key], axis=1),
                query,
                (((1,), (1,)), ((), ())),
                preferred_element_type=jnp.float32,
            )
            scores_ref[c * KC : (c + 1) * KC, :] = scores
            for b in range(KC // BLOCK):
                most = jnp.max(scores[b * BLOCK : (b + 1) * BLOCK].reshape(-1, 8, TQ), axis=0)
                top = jnp.maximum(top, choose(c * (KC // BLOCK) + b, most, -BIG))
        top = jnp.max(top, axis=0, keepdims=True)
        mixed = jnp.zeros((HD + 16, TQ), jnp.float32)
        for c in range(length // KC):
            parts = []
            for b in range(KC // BLOCK):
                j = c * (KC // BLOCK) + b
                shift = choose(j, top, BIG)
                parts.append(
                    jnp.exp2(scores_ref[j * BLOCK : (j + 1) * BLOCK, :] - shift).astype(jnp.bfloat16)
                )
            mixed = mixed + jnp.dot(
                value_ref[:, c * KC : (c + 1) * KC],
                jnp.concatenate(parts, axis=0),
                preferred_element_type=jnp.float32,
            )
        result = mixed[0:HD] * (1.0 / mixed[HD : HD + 1])
        put(tile, start, result.T.astype(jnp.bfloat16))

    pl.loop(0, tiles)(step)


def kernel(
    queries,
    keys,
    values,
    spatial_mask,
    temporal_mask,
    out,
    s_in,
    t_in,
    s_out,
    t_out,
    s_mask_in,
    t_mask_in,
    s_mask,
    t_mask,
    scores_ref,
    value_ref,
    mask_sem,
    in_recv,
    s_send,
    t_send,
    s_out_send,
    t_out_send,
    out_recv,
):
    me_f = lax.axis_index("frame")
    me_p = lax.axis_index("patch")
    tensors = (queries, keys, values)

    mask_copies = (
        pltpu.make_async_copy(
            spatial_mask.at[pl.ds(lax.rem(me_p, 4) * ITEMS_S, ITEMS_S)], s_mask_in, mask_sem.at[0]
        ),
        pltpu.make_async_copy(
            temporal_mask.at[pl.ds(lax.rem(me_f, 2) * ITEMS_T, ITEMS_T)], t_mask_in, mask_sem.at[1]
        ),
    )
    for copy in mask_copies:
        copy.start()

    barrier = pltpu.get_barrier_semaphore()

    @pl.loop(1, NP)
    def _(d):
        pl.semaphore_signal(
            barrier, inc=1, device_id=(me_f, lax.rem(me_p + d, NP)), device_id_type=MESH
        )

    @pl.loop(1, NF)
    def _(d):
        pl.semaphore_signal(
            barrier, inc=1, device_id=(lax.rem(me_f + d, NF), me_p), device_id_type=MESH
        )

    pl.semaphore_wait(barrier, NP + NF - 2)

    def spatial_place(rank, n):
        item = rank * ITEMS_S + n
        frame = item // SH
        return frame, pl.multiple_of((item - frame * SH) * HD, HD)

    def temporal_place(rank, c):
        group = rank // 2
        head = SH + (rank - group * 2) * ITEMS_T + c * CHUNK
        return pl.multiple_of(group * GP, GP), pl.multiple_of(head * HD, HD)

    def is_temporal(s):
        return lax.rem(s, 4) == 1

    def spatial_index(s):
        return s - (s + 2) // 4

    def start_spatial(s):
        n = spatial_index(s)

        def parts(rank):
            frame, column = spatial_place(rank, n)
            for i, tensor in enumerate(tensors):
                yield (
                    tensor.at[frame, :, pl.ds(column, HD)],
                    s_in.at[n, pl.ds(pl.multiple_of(i * SEQ_S + me_p * CELLS, CELLS), CELLS)],
                )

        @pl.loop(1, NP)
        def _(d):
            rank = lax.rem(me_p + d, NP)
            for source, target in parts(rank):
                pltpu.make_async_remote_copy(
                    src_ref=source,
                    dst_ref=target,
                    send_sem=s_send,
                    recv_sem=in_recv.at[s],
                    device_id=(me_f, rank),
                    device_id_type=MESH,
                ).start()

        for source, target in parts(me_p):
            pltpu.make_async_copy(source, target, in_recv.at[s]).start()

    def start_temporal(s):
        c = s // 4

        def parts(rank):
            row, column = temporal_place(rank, c)
            for i, tensor in enumerate(tensors):
                yield (
                    tensor.at[:, pl.ds(row, GP), pl.ds(column, CW)],
                    t_in.at[c, pl.ds(i * NF * FD + me_f * FD, FD)],
                )

        @pl.loop(1, NF)
        def _(d):
            rank = lax.rem(me_f + d, NF)
            for source, target in parts(rank):
                pltpu.make_async_remote_copy(
                    src_ref=source,
                    dst_ref=target,
                    send_sem=t_send,
                    recv_sem=in_recv.at[s],
                    device_id=(rank, me_p),
                    device_id_type=MESH,
                ).start()

        for source, target in parts(me_f):
            pltpu.make_async_copy(source, target, in_recv.at[s]).start()

    def start_stage(s):
        @pl.when(is_temporal(s))
        def _():
            start_temporal(s)

        @pl.when(jnp.logical_not(is_temporal(s)))
        def _():
            start_spatial(s)

    pl.loop(0, AHEAD)(start_stage)

    for copy in mask_copies:
        copy.wait()
    s_lane = me_f * FD + me_p // 4
    t_lane = me_p * (CELLS // GP) + me_f // 2

    def spread(rows, lane):
        lanes = lax.broadcasted_iota(jnp.int32, rows.shape, 2)
        chosen = jnp.sum(jnp.where(lanes == lane, rows.astype(jnp.float32), 0.0), axis=2, keepdims=True)
        return jnp.broadcast_to(chosen, rows.shape[:2] + (BLOCK,))

    @pl.loop(0, ITEMS_S)
    def _(n):
        s_mask[pl.ds(n * NB_S, NB_S)] = spread(s_mask_in[n], s_lane)

    @pl.loop(0, ITEMS_T)
    def _(n):
        t_mask[pl.ds(n * NB_T, NB_T)] = spread(t_mask_in[n], t_lane)

    value_ref[HD:, :] = jnp.ones((16, SEQ_S), jnp.bfloat16)

    def work_spatial(s):
        n = spatial_index(s)
        frame, column = spatial_place(me_p, n)
        pltpu.make_async_copy(s_in.at[n], s_in.at[n], in_recv.at[s]).wait()

        def put(tile, start, rows):
            s_out[n, pl.ds(start, TQ), :] = rows
            source = s_out.at[n, pl.ds(start, TQ)]
            target = out.at[frame, :, pl.ds(column, HD)]

            @pl.when(tile != me_p)
            def _():
                pltpu.make_async_remote_copy(
                    src_ref=source,
                    dst_ref=target,
                    send_sem=s_out_send,
                    recv_sem=out_recv,
                    device_id=(me_f, tile),
                    device_id_type=MESH,
                ).start()

            @pl.when(tile == me_p)
            def _():
                pltpu.make_async_copy(source, target, out_recv).start()

        attend(
            lambda a, l: s_in[n, pl.ds(a, l), :],
            lambda a, l: s_in[n, pl.ds(SEQ_S + a, l), :],
            lambda a, l: s_in[n, pl.ds(2 * SEQ_S + a, l), :],
            lambda i, j: s_mask[n * NB_S + i, j : j + 1, :],
            put,
            me_p + 1,
            SEQ_S,
            scores_ref,
            value_ref,
        )

    def work_temporal(s):
        c = s // 4
        pltpu.make_async_copy(t_in.at[c], t_in.at[c], in_recv.at[s]).wait()
        row, column = temporal_place(me_f, c)
        ranks = TQ // (FD * GP)

        @pl.loop(0, CHUNK)
        def _(h):
            lanes = pl.ds(pl.multiple_of(h * HD, HD), HD)

            def get(i):
                def rows(a, l):
                    if isinstance(a, int):
                        first = a // GP
                    else:
                        first = a // GP
                    return t_in[c, pl.ds(i * NF * FD + first, l // GP), :, lanes].reshape(l, HD)

                return rows

            def put(tile, start, rows):
                frame = tile * (TQ // GP)
                t_out[c, pl.ds(frame, TQ // GP), :, lanes] = rows.reshape(TQ // GP, GP, HD)
                target = out.at[
                    :, pl.ds(row, GP), pl.ds(pl.multiple_of(column + h * HD, HD), HD)
                ]

                for e in range(ranks):
                    rank = tile * ranks + e
                    source = t_out.at[c, pl.ds(rank * FD, FD), :, lanes]

                    @pl.when(rank != me_f)
                    def _():
                        pltpu.make_async_remote_copy(
                            src_ref=source,
                            dst_ref=target,
                            send_sem=t_out_send,
                            recv_sem=out_recv,
                            device_id=(rank, me_p),
                            device_id_type=MESH,
                        ).start()

                    @pl.when(rank == me_f)
                    def _():
                        pltpu.make_async_copy(source, target, out_recv).start()

            item = (c * CHUNK + h) * NB_T
            attend(
                get(0),
                get(1),
                get(2),
                lambda i, j: t_mask[item + i, j : j + 1, :],
                put,
                me_f // ranks + 1,
                SEQ_T,
                scores_ref,
                value_ref,
            )

    @pl.loop(0, STAGES)
    def _(s):
        @pl.when(s + AHEAD < STAGES)
        def _():
            start_stage(s + AHEAD)

        @pl.when(is_temporal(s))
        def _():
            work_temporal(s)

        @pl.when(jnp.logical_not(is_temporal(s)))
        def _():
            work_spatial(s)

    sent = (
        (s_in.at[:, pl.ds(0, 3 * (NP - 1) * CELLS)], s_send),
        (t_in.at[:, pl.ds(0, 3 * (NF - 1) * FD)], t_send),
        (s_out.at[:, pl.ds(0, (NP - 1) * CELLS)], s_out_send),
        (t_out.at[:, pl.ds(0, (NF - 1) * FD)], t_out_send),
        (out, out_recv),
    )
    for ref, sem in sent:
        pltpu.make_async_copy(ref, ref, sem).wait()


def shards(queries, keys, values, spatial_mask, temporal_mask):
    anywhere = pl.BlockSpec(memory_space=pl.ANY)
    dma = pltpu.SemaphoreType.DMA
    flops = 4 * HD * (ITEMS_S * SEQ_S**2 + ITEMS_T * SEQ_T**2)
    return pl.pallas_call(
        kernel,
        out_shape=jax.ShapeDtypeStruct(queries.shape, queries.dtype),
        in_specs=[anywhere] * 5,
        out_specs=anywhere,
        scratch_shapes=[
            pltpu.VMEM((ITEMS_S, 3 * SEQ_S, HD), jnp.bfloat16),
            pltpu.VMEM((CHUNKS, 3 * NF * FD, GP, CW), jnp.bfloat16),
            pltpu.VMEM((ITEMS_S, SEQ_S, HD), jnp.bfloat16),
            pltpu.VMEM((CHUNKS, NF * FD, GP, CW), jnp.bfloat16),
            pltpu.VMEM((ITEMS_S, NB_S, NB_S, 32), jnp.int32),
            pltpu.VMEM((ITEMS_T, NB_T, NB_T, 64), jnp.int32),
            pltpu.VMEM((ITEMS_S * NB_S, NB_S, BLOCK), jnp.float32),
            pltpu.VMEM((ITEMS_T * NB_T, NB_T, BLOCK), jnp.float32),
            pltpu.VMEM((SEQ_S, TQ), jnp.float32),
            pltpu.VMEM((HD + 16, SEQ_S), jnp.bfloat16),
            dma((2,)),
            dma((STAGES,)),
            dma,
            dma,
            dma,
            dma,
            dma,
        ],
        compiler_params=pltpu.CompilerParams(
            collective_id=0, has_side_effects=True, vmem_limit_bytes=60 * 2**20
        ),
        cost_estimate=pl.CostEstimate(
            flops=flops, bytes_accessed=4 * queries.size * 2, transcendentals=flops // (4 * HD)
        ),
    )(
        queries,
        keys,
        values,
        spatial_mask.transpose(1, 2, 3, 0),
        temporal_mask.transpose(1, 2, 3, 0),
    )


def solution(mesh):
    in_specs = (
        P("frame", "patch", None),
        P("frame", "patch", None),
        P("frame", "patch", None),
        P(),
        P(),
    )
    out_specs = P("frame", "patch", None)
    return jax.shard_map(shards, mesh=mesh, in_specs=in_specs, out_specs=out_specs, check_vma=False)
```

```python
import functools
import math

import jax
import jax.numpy as jnp
from jax import lax
from jax.experimental import pallas as pl
from jax.experimental.pallas import tpu as pltpu
from jax.sharding import PartitionSpec as P

HD = 128
SH = 28
TH = 12
GP = 32
BLOCK = 128
NF = 16
NP = 8
FD = 2
CELLS = 256
SEQ_S = NP * CELLS
SEQ_T = NF * FD * GP
NB_S = SEQ_S // BLOCK
NB_T = SEQ_T // BLOCK
ITEMS_S = FD * SH // NP
ITEMS_T = (CELLS // GP) * TH // NF
CHUNK = 2
CHUNKS = ITEMS_T // CHUNK
CW = CHUNK * HD
STAGES = ITEMS_S + CHUNKS
AHEAD = 5
TQ = 256
KC = 256
UNITS = 1.0 / math.sqrt(HD) * math.log2(math.e)
BIG = 1e30
MESH = pl.DeviceIdType.MESH


def attend(get_query, get_key, get_value, get_mask, put, first, length, scores_ref, value_ref):
    tiles = length // TQ
    halves = TQ // BLOCK
    for c in range(length // KC):
        value_ref[0:HD, c * KC : (c + 1) * KC] = get_value(c * KC, KC).T

    def step(d):
        tile = lax.rem(first + d, tiles)
        start = pl.multiple_of(tile * TQ, TQ)
        scaled = get_query(start, TQ).astype(jnp.float32) * UNITS
        high = scaled.astype(jnp.bfloat16)
        low = (scaled - high.astype(jnp.float32)).astype(jnp.bfloat16)
        query = jnp.concatenate([high, low], axis=1)

        def choose(j, rows, otherwise):
            parts = [
                jnp.where(
                    get_mask(tile * halves + i, j) > 0,
                    rows[:, i * BLOCK : (i + 1) * BLOCK],
                    otherwise,
                )
                for i in range(halves)
            ]
            return jnp.concatenate(parts, axis=1)

        top = jnp.full((8, TQ), -BIG, jnp.float32)
        for c in range(length // KC):
            key = get_key(c * KC, KC)
            scores = lax.dot_general(
                jnp.concatenate([key, key], axis=1),
                query,
                (((1,), (1,)), ((), ())),
                preferred_element_type=jnp.float32,
            )
            scores_ref[c * KC : (c + 1) * KC, :] = scores
            for b in range(KC // BLOCK):
                most = jnp.max(scores[b * BLOCK : (b + 1) * BLOCK].reshape(-1, 8, TQ), axis=0)
                top = jnp.maximum(top, choose(c * (KC // BLOCK) + b, most, -BIG))
        top = jnp.max(top, axis=0, keepdims=True)
        mixed = jnp.zeros((HD + 16, TQ), jnp.float32)
        for c in range(length // KC):
            parts = []
            for b in range(KC // BLOCK):
                j = c * (KC // BLOCK) + b
                shift = choose(j, top, BIG)
                parts.append(
                    jnp.exp2(scores_ref[j * BLOCK : (j + 1) * BLOCK, :] - shift).astype(jnp.bfloat16)
                )
            mixed = mixed + jnp.dot(
                value_ref[:, c * KC : (c + 1) * KC],
                jnp.concatenate(parts, axis=0),
                preferred_element_type=jnp.float32,
            )
        result = mixed[0:HD] * (1.0 / mixed[HD : HD + 1])
        put(tile, start, result.T.astype(jnp.bfloat16))

    pl.loop(0, tiles)(step)


def kernel(
    queries,
    keys,
    values,
    spatial_mask,
    temporal_mask,
    out,
    s_in,
    t_in,
    s_out,
    t_out,
    s_mask_in,
    t_mask_in,
    s_mask,
    t_mask,
    scores_ref,
    value_ref,
    mask_sem,
    in_recv,
    s_send,
    t_send,
    s_out_send,
    t_out_send,
    out_recv,
):
    me_f = lax.axis_index("frame")
    me_p = lax.axis_index("patch")
    tensors = (queries, keys, values)

    mask_copies = (
        pltpu.make_async_copy(
            spatial_mask.at[pl.ds(lax.rem(me_p, 4) * ITEMS_S, ITEMS_S)], s_mask_in, mask_sem.at[0]
        ),
        pltpu.make_async_copy(
            temporal_mask.at[pl.ds(lax.rem(me_f, 2) * ITEMS_T, ITEMS_T)], t_mask_in, mask_sem.at[1]
        ),
    )
    for copy in mask_copies:
        copy.start()

    barrier = pltpu.get_barrier_semaphore()

    @pl.loop(1, NP)
    def _(d):
        pl.semaphore_signal(
            barrier, inc=1, device_id=(me_f, lax.rem(me_p + d, NP)), device_id_type=MESH
        )

    @pl.loop(1, NF)
    def _(d):
        pl.semaphore_signal(
            barrier, inc=1, device_id=(lax.rem(me_f + d, NF), me_p), device_id_type=MESH
        )

    pl.semaphore_wait(barrier, NP + NF - 2)

    def spatial_place(rank, n):
        item = rank * ITEMS_S + n
        frame = item // SH
        return frame, pl.multiple_of((item - frame * SH) * HD, HD)

    def temporal_place(rank, c):
        group = rank // 2
        head = SH + (rank - group * 2) * ITEMS_T + c * CHUNK
        return pl.multiple_of(group * GP, GP), pl.multiple_of(head * HD, HD)

    def is_temporal(s):
        return lax.rem(s, 4) == 1

    def spatial_index(s):
        return s - (s + 2) // 4

    def start_spatial(s):
        n = spatial_index(s)

        def parts(rank):
            frame, column = spatial_place(rank, n)
            for i, tensor in enumerate(tensors):
                yield (
                    tensor.at[frame, :, pl.ds(column, HD)],
                    s_in.at[n, pl.ds(pl.multiple_of(i * SEQ_S + me_p * CELLS, CELLS), CELLS)],
                )

        @pl.loop(1, NP)
        def _(d):
            rank = lax.rem(me_p + d, NP)
            for source, target in parts(rank):
                pltpu.make_async_remote_copy(
                    src_ref=source,
                    dst_ref=target,
                    send_sem=s_send,
                    recv_sem=in_recv.at[s],
                    device_id=(me_f, rank),
                    device_id_type=MESH,
                ).start()

        for source, target in parts(me_p):
            pltpu.make_async_copy(source, target, in_recv.at[s]).start()

    def start_temporal(s):
        c = s // 4

        def parts(rank):
            row, column = temporal_place(rank, c)
            for i, tensor in enumerate(tensors):
                yield (
                    tensor.at[:, pl.ds(row, GP), pl.ds(column, CW)],
                    t_in.at[c, pl.ds(i * NF * FD + me_f * FD, FD)],
                )

        @pl.loop(1, NF)
        def _(d):
            rank = lax.rem(me_f + d, NF)
            for source, target in parts(rank):
                pltpu.make_async_remote_copy(
                    src_ref=source,
                    dst_ref=target,
                    send_sem=t_send,
                    recv_sem=in_recv.at[s],
                    device_id=(rank, me_p),
                    device_id_type=MESH,
                ).start()

        for source, target in parts(me_f):
            pltpu.make_async_copy(source, target, in_recv.at[s]).start()

    def start_stage(s):
        @pl.when(is_temporal(s))
        def _():
            start_temporal(s)

        @pl.when(jnp.logical_not(is_temporal(s)))
        def _():
            start_spatial(s)

    pl.loop(0, AHEAD)(start_stage)

    for copy in mask_copies:
        copy.wait()
    s_lane = me_f * FD + me_p // 4
    t_lane = me_p * (CELLS // GP) + me_f // 2

    def spread(rows, lane):
        lanes = lax.broadcasted_iota(jnp.int32, rows.shape, 2)
        chosen = jnp.sum(jnp.where(lanes == lane, rows.astype(jnp.float32), 0.0), axis=2, keepdims=True)
        return jnp.broadcast_to(chosen, rows.shape[:2] + (BLOCK,))

    @pl.loop(0, ITEMS_S)
    def _(n):
        s_mask[pl.ds(n * NB_S, NB_S)] = spread(s_mask_in[n], s_lane)

    @pl.loop(0, ITEMS_T)
    def _(n):
        t_mask[pl.ds(n * NB_T, NB_T)] = spread(t_mask_in[n], t_lane)

    value_ref[HD:, :] = jnp.ones((16, SEQ_S), jnp.bfloat16)

    def work_spatial(s):
        n = spatial_index(s)
        frame, column = spatial_place(me_p, n)
        pltpu.make_async_copy(s_in.at[n], s_in.at[n], in_recv.at[s]).wait()

        def put(tile, start, rows):
            s_out[n, pl.ds(start, TQ), :] = rows
            source = s_out.at[n, pl.ds(start, TQ)]
            target = out.at[frame, :, pl.ds(column, HD)]

            @pl.when(tile != me_p)
            def _():
                pltpu.make_async_remote_copy(
                    src_ref=source,
                    dst_ref=target,
                    send_sem=s_out_send,
                    recv_sem=out_recv,
                    device_id=(me_f, tile),
                    device_id_type=MESH,
                ).start()

            @pl.when(tile == me_p)
            def _():
                pltpu.make_async_copy(source, target, out_recv).start()

        attend(
            lambda a, l: s_in[n, pl.ds(a, l), :],
            lambda a, l: s_in[n, pl.ds(SEQ_S + a, l), :],
            lambda a, l: s_in[n, pl.ds(2 * SEQ_S + a, l), :],
            lambda i, j: s_mask[n * NB_S + i, j : j + 1, :],
            put,
            me_p + 1,
            SEQ_S,
            scores_ref,
            value_ref,
        )

    def work_temporal(s):
        c = s // 4
        pltpu.make_async_copy(t_in.at[c], t_in.at[c], in_recv.at[s]).wait()
        row, column = temporal_place(me_f, c)
        ranks = TQ // (FD * GP)

        @pl.loop(0, CHUNK)
        def _(h):
            lanes = pl.ds(pl.multiple_of(h * HD, HD), HD)

            def get(i):
                def rows(a, l):
                    if isinstance(a, int):
                        first = a // GP
                    else:
                        first = a // GP
                    return t_in[c, pl.ds(i * NF * FD + first, l // GP), :, lanes].reshape(l, HD)

                return rows

            def put(tile, start, rows):
                frame = tile * (TQ // GP)
                t_out[c, pl.ds(frame, TQ // GP), :, lanes] = rows.reshape(TQ // GP, GP, HD)
                target = out.at[
                    :, pl.ds(row, GP), pl.ds(pl.multiple_of(column + h * HD, HD), HD)
                ]

                for e in range(ranks):
                    rank = tile * ranks + e
                    source = t_out.at[c, pl.ds(rank * FD, FD), :, lanes]

                    @pl.when(rank != me_f)
                    def _():
                        pltpu.make_async_remote_copy(
                            src_ref=source,
                            dst_ref=target,
                            send_sem=t_out_send,
                            recv_sem=out_recv,
                            device_id=(rank, me_p),
                            device_id_type=MESH,
                        ).start()

                    @pl.when(rank == me_f)
                    def _():
                        pltpu.make_async_copy(source, target, out_recv).start()

            item = (c * CHUNK + h) * NB_T
            attend(
                get(0),
                get(1),
                get(2),
                lambda i, j: t_mask[item + i, j : j + 1, :],
                put,
                me_f // ranks + 1,
                SEQ_T,
                scores_ref,
                value_ref,
            )

    @pl.loop(0, STAGES)
    def _(s):
        @pl.when(s + AHEAD < STAGES)
        def _():
            start_stage(s + AHEAD)

        @pl.when(is_temporal(s))
        def _():
            work_temporal(s)

        @pl.when(jnp.logical_not(is_temporal(s)))
        def _():
            work_spatial(s)

    sent = (
        (s_in.at[:, pl.ds(0, 3 * (NP - 1) * CELLS)], s_send),
        (t_in.at[:, pl.ds(0, 3 * (NF - 1) * FD)], t_send),
        (s_out.at[:, pl.ds(0, (NP - 1) * CELLS)], s_out_send),
        (t_out.at[:, pl.ds(0, (NF - 1) * FD)], t_out_send),
        (out, out_recv),
    )
    for ref, sem in sent:
        pltpu.make_async_copy(ref, ref, sem).wait()


def shards(queries, keys, values, spatial_mask, temporal_mask):
    anywhere = pl.BlockSpec(memory_space=pl.ANY)
    held = pl.BlockSpec(memory_space=pltpu.HBM)
    dma = pltpu.SemaphoreType.DMA
    flops = 4 * HD * (ITEMS_S * SEQ_S**2 + ITEMS_T * SEQ_T**2)
    return pl.pallas_call(
        kernel,
        out_shape=pltpu.VMEM(queries.shape, queries.dtype),
        in_specs=[held] * 5,
        out_specs=anywhere,
        scratch_shapes=[
            pltpu.VMEM((ITEMS_S, 3 * SEQ_S, HD), jnp.bfloat16),
            pltpu.VMEM((CHUNKS, 3 * NF * FD, GP, CW), jnp.bfloat16),
            pltpu.VMEM((ITEMS_S, SEQ_S, HD), jnp.bfloat16),
            pltpu.VMEM((CHUNKS, NF * FD, GP, CW), jnp.bfloat16),
            pltpu.VMEM((ITEMS_S, NB_S, NB_S, 32), jnp.int32),
            pltpu.VMEM((ITEMS_T, NB_T, NB_T, 64), jnp.int32),
            pltpu.VMEM((ITEMS_S * NB_S, NB_S, BLOCK), jnp.float32),
            pltpu.VMEM((ITEMS_T * NB_T, NB_T, BLOCK), jnp.float32),
            pltpu.VMEM((SEQ_S, TQ), jnp.float32),
            pltpu.VMEM((HD + 16, SEQ_S), jnp.bfloat16),
            dma((2,)),
            dma((STAGES,)),
            dma,
            dma,
            dma,
            dma,
            dma,
        ],
        compiler_params=pltpu.CompilerParams(
            collective_id=0, has_side_effects=True, vmem_limit_bytes=50 * 2**20
        ),
        cost_estimate=pl.CostEstimate(
            flops=flops, bytes_accessed=4 * queries.size * 2, transcendentals=flops // (4 * HD)
        ),
    )(
        queries,
        keys,
        values,
        spatial_mask.transpose(1, 2, 3, 0),
        temporal_mask.transpose(1, 2, 3, 0),
    )


def solution(mesh):
    in_specs = (
        P("frame", "patch", None),
        P("frame", "patch", None),
        P("frame", "patch", None),
        P(),
        P(),
    )
    out_specs = P("frame", "patch", None)
    return jax.shard_map(shards, mesh=mesh, in_specs=in_specs, out_specs=out_specs, check_vma=False)
```

```python
import functools
import math

import jax
import jax.numpy as jnp
from jax import lax
from jax.experimental import pallas as pl
from jax.experimental.pallas import tpu as pltpu
from jax.sharding import PartitionSpec as P

HD = 128
SH = 28
TH = 12
GP = 32
BLOCK = 128
NF = 16
NP = 8
FD = 2
CELLS = 256
SEQ_S = NP * CELLS
SEQ_T = NF * FD * GP
NB_S = SEQ_S // BLOCK
NB_T = SEQ_T // BLOCK
ITEMS_S = FD * SH // NP
ITEMS_T = (CELLS // GP) * TH // NF
CHUNK = 2
CHUNKS = ITEMS_T // CHUNK
CW = CHUNK * HD
STAGES = ITEMS_S + CHUNKS
HOLD = 4
AHEAD = 5
TQ = 256
KC = 256
UNITS = 1.0 / math.sqrt(HD) * math.log2(math.e)
BIG = 1e30
MESH = pl.DeviceIdType.MESH


def attend(get_query, get_key, get_value, get_mask, put, first, length, scores_ref, value_ref):
    tiles = length // TQ
    halves = TQ // BLOCK
    for c in range(length // KC):
        value_ref[0:HD, c * KC : (c + 1) * KC] = get_value(c * KC, KC).T

    def step(d):
        tile = lax.rem(first + d, tiles)
        start = pl.multiple_of(tile * TQ, TQ)
        scaled = get_query(start, TQ).astype(jnp.float32) * UNITS
        high = scaled.astype(jnp.bfloat16)
        low = (scaled - high.astype(jnp.float32)).astype(jnp.bfloat16)
        query = jnp.concatenate([high, low], axis=1)

        def choose(j, rows, otherwise):
            parts = [
                jnp.where(
                    get_mask(tile * halves + i, j) > 0,
                    rows[:, i * BLOCK : (i + 1) * BLOCK],
                    otherwise,
                )
                for i in range(halves)
            ]
            return jnp.concatenate(parts, axis=1)

        top = jnp.full((8, TQ), -BIG, jnp.float32)
        for c in range(length // KC):
            key = get_key(c * KC, KC)
            scores = lax.dot_general(
                jnp.concatenate([key, key], axis=1),
                query,
                (((1,), (1,)), ((), ())),
                preferred_element_type=jnp.float32,
            )
            scores_ref[c * KC : (c + 1) * KC, :] = scores
            for b in range(KC // BLOCK):
                most = jnp.max(scores[b * BLOCK : (b + 1) * BLOCK].reshape(-1, 8, TQ), axis=0)
                top = jnp.maximum(top, choose(c * (KC // BLOCK) + b, most, -BIG))
        top = jnp.max(top, axis=0, keepdims=True)
        mixed = jnp.zeros((HD + 16, TQ), jnp.float32)
        for c in range(length // KC):
            parts = []
            for b in range(KC // BLOCK):
                j = c * (KC // BLOCK) + b
                shift = choose(j, top, BIG)
                parts.append(
                    jnp.exp2(scores_ref[j * BLOCK : (j + 1) * BLOCK, :] - shift).astype(jnp.bfloat16)
                )
            mixed = mixed + jnp.dot(
                value_ref[:, c * KC : (c + 1) * KC],
                jnp.concatenate(parts, axis=0),
                preferred_element_type=jnp.float32,
            )
        result = mixed[0:HD] * (1.0 / mixed[HD : HD + 1])
        put(tile, start, result.T.astype(jnp.bfloat16))

    pl.loop(0, tiles)(step)


def kernel(
    queries,
    keys,
    values,
    spatial_mask,
    temporal_mask,
    out,
    s_in,
    t_in,
    s_out,
    t_out,
    s_mask_in,
    t_mask_in,
    s_mask,
    t_mask,
    scores_ref,
    value_ref,
    mask_sem,
    in_recv,
    s_send,
    t_send,
    s_out_send,
    t_out_send,
    out_recv,
):
    me_f = lax.axis_index("frame")
    me_p = lax.axis_index("patch")
    tensors = (queries, keys, values)

    mask_copies = (
        pltpu.make_async_copy(
            spatial_mask.at[pl.ds(lax.rem(me_p, 4) * ITEMS_S, ITEMS_S)], s_mask_in, mask_sem.at[0]
        ),
        pltpu.make_async_copy(
            temporal_mask.at[pl.ds(lax.rem(me_f, 2) * ITEMS_T, ITEMS_T)], t_mask_in, mask_sem.at[1]
        ),
    )
    for copy in mask_copies:
        copy.start()

    barrier = pltpu.get_barrier_semaphore()

    @pl.loop(1, NP)
    def _(d):
        pl.semaphore_signal(
            barrier, inc=1, device_id=(me_f, lax.rem(me_p + d, NP)), device_id_type=MESH
        )

    @pl.loop(1, NF)
    def _(d):
        pl.semaphore_signal(
            barrier, inc=1, device_id=(lax.rem(me_f + d, NF), me_p), device_id_type=MESH
        )

    pl.semaphore_wait(barrier, NP + NF - 2)

    def spatial_place(rank, n):
        item = rank * ITEMS_S + n
        frame = item // SH
        return frame, pl.multiple_of((item - frame * SH) * HD, HD)

    def temporal_place(rank, c):
        group = rank // 2
        head = SH + (rank - group * 2) * ITEMS_T + c * CHUNK
        return pl.multiple_of(group * GP, GP), pl.multiple_of(head * HD, HD)

    def is_temporal(s):
        return lax.rem(s, 4) == 1

    def spatial_index(s):
        return s - (s + 2) // 4

    def start_spatial(s):
        n = spatial_index(s)

        def parts(rank):
            frame, column = spatial_place(rank, n)
            for i, tensor in enumerate(tensors):
                yield (
                    tensor.at[frame, :, pl.ds(column, HD)],
                    s_in.at[n, pl.ds(pl.multiple_of(i * SEQ_S + me_p * CELLS, CELLS), CELLS)],
                )

        @pl.loop(1, NP)
        def _(d):
            rank = lax.rem(me_p + d, NP)
            for source, target in parts(rank):
                pltpu.make_async_remote_copy(
                    src_ref=source,
                    dst_ref=target,
                    send_sem=s_send,
                    recv_sem=in_recv.at[s],
                    device_id=(me_f, rank),
                    device_id_type=MESH,
                ).start()

        for source, target in parts(me_p):
            pltpu.make_async_copy(source, target, in_recv.at[s]).start()

    def start_temporal(s):
        c = s // 4

        def parts(rank):
            row, column = temporal_place(rank, c)
            for i, tensor in enumerate(tensors):
                yield (
                    tensor.at[:, pl.ds(row, GP), pl.ds(column, CW)],
                    t_in.at[c, pl.ds(i * NF * FD + me_f * FD, FD)],
                )

        @pl.loop(1, NF)
        def _(d):
            rank = lax.rem(me_f + d, NF)
            for source, target in parts(rank):
                pltpu.make_async_remote_copy(
                    src_ref=source,
                    dst_ref=target,
                    send_sem=t_send,
                    recv_sem=in_recv.at[s],
                    device_id=(rank, me_p),
                    device_id_type=MESH,
                ).start()

        for source, target in parts(me_f):
            pltpu.make_async_copy(source, target, in_recv.at[s]).start()

    def start_stage(s):
        @pl.when(is_temporal(s))
        def _():
            start_temporal(s)

        @pl.when(jnp.logical_not(is_temporal(s)))
        def _():
            start_spatial(s)

    pl.loop(0, AHEAD)(start_stage)

    for copy in mask_copies:
        copy.wait()
    s_lane = me_f * FD + me_p // 4
    t_lane = me_p * (CELLS // GP) + me_f // 2

    def spread(rows, lane):
        lanes = lax.broadcasted_iota(jnp.int32, rows.shape, 2)
        chosen = jnp.sum(jnp.where(lanes == lane, rows.astype(jnp.float32), 0.0), axis=2, keepdims=True)
        return jnp.broadcast_to(chosen, rows.shape[:2] + (BLOCK,))

    @pl.loop(0, ITEMS_S)
    def _(n):
        s_mask[pl.ds(n * NB_S, NB_S)] = spread(s_mask_in[n], s_lane)

    @pl.loop(0, ITEMS_T)
    def _(n):
        t_mask[pl.ds(n * NB_T, NB_T)] = spread(t_mask_in[n], t_lane)

    value_ref[HD:, :] = jnp.ones((16, SEQ_S), jnp.bfloat16)

    beside = me_p + 1 - 2 * lax.rem(me_p, 2)

    def spatial_rows(n, rank):
        frame, column = spatial_place(me_p, n)
        return (
            s_out.at[n, pl.ds(pl.multiple_of(rank * CELLS, CELLS), CELLS)],
            out.at[frame, :, pl.ds(column, HD)],
        )

    def give_spatial(n, rank):
        source, target = spatial_rows(n, rank)
        pltpu.make_async_remote_copy(
            src_ref=source,
            dst_ref=target,
            send_sem=s_out_send,
            recv_sem=out_recv,
            device_id=(me_f, rank),
            device_id_type=MESH,
        ).start()

    def work_spatial(s):
        n = spatial_index(s)
        pltpu.make_async_copy(s_in.at[n], s_in.at[n], in_recv.at[s]).wait()

        def put(tile, start, rows):
            s_out[n, pl.ds(start, TQ), :] = rows
            held = (tile == beside) & (n >= ITEMS_S - HOLD)

            @pl.when((tile != me_p) & jnp.logical_not(held))
            def _():
                give_spatial(n, tile)

            @pl.when(tile == me_p)
            def _():
                source, target = spatial_rows(n, tile)
                pltpu.make_async_copy(source, target, out_recv).start()

        attend(
            lambda a, l: s_in[n, pl.ds(a, l), :],
            lambda a, l: s_in[n, pl.ds(SEQ_S + a, l), :],
            lambda a, l: s_in[n, pl.ds(2 * SEQ_S + a, l), :],
            lambda i, j: s_mask[n * NB_S + i, j : j + 1, :],
            put,
            me_p + 1,
            SEQ_S,
            scores_ref,
            value_ref,
        )

    def work_temporal(s):
        c = s // 4
        pltpu.make_async_copy(t_in.at[c], t_in.at[c], in_recv.at[s]).wait()
        row, column = temporal_place(me_f, c)
        ranks = TQ // (FD * GP)

        @pl.loop(0, CHUNK)
        def _(h):
            lanes = pl.ds(pl.multiple_of(h * HD, HD), HD)

            def get(i):
                def rows(a, l):
                    return t_in[c, pl.ds(i * NF * FD + a // GP, l // GP), :, lanes].reshape(l, HD)

                return rows

            def put(tile, start, rows):
                frame = tile * (TQ // GP)
                t_out[c, pl.ds(frame, TQ // GP), :, lanes] = rows.reshape(TQ // GP, GP, HD)
                target = out.at[
                    :, pl.ds(row, GP), pl.ds(pl.multiple_of(column + h * HD, HD), HD)
                ]

                for e in range(ranks):
                    rank = tile * ranks + e
                    source = t_out.at[c, pl.ds(rank * FD, FD), :, lanes]

                    @pl.when(rank != me_f)
                    def _():
                        pltpu.make_async_remote_copy(
                            src_ref=source,
                            dst_ref=target,
                            send_sem=t_out_send,
                            recv_sem=out_recv,
                            device_id=(rank, me_p),
                            device_id_type=MESH,
                        ).start()

                    @pl.when(rank == me_f)
                    def _():
                        pltpu.make_async_copy(source, target, out_recv).start()

            item = (c * CHUNK + h) * NB_T
            attend(
                get(0),
                get(1),
                get(2),
                lambda i, j: t_mask[item + i, j : j + 1, :],
                put,
                me_f // ranks + 1,
                SEQ_T,
                scores_ref,
                value_ref,
            )

    @pl.loop(0, STAGES)
    def _(s):
        @pl.when(s + AHEAD < STAGES)
        def _():
            start_stage(s + AHEAD)

        @pl.when(is_temporal(s))
        def _():
            work_temporal(s)

        @pl.when(jnp.logical_not(is_temporal(s)))
        def _():
            work_spatial(s)

    @pl.loop(ITEMS_S - HOLD, ITEMS_S)
    def _(n):
        give_spatial(n, beside)

    sent = (
        (s_in.at[:, pl.ds(0, 3 * (NP - 1) * CELLS)], s_send),
        (t_in.at[:, pl.ds(0, 3 * (NF - 1) * FD)], t_send),
        (s_out.at[:, pl.ds(0, (NP - 1) * CELLS)], s_out_send),
        (t_out.at[:, pl.ds(0, (NF - 1) * FD)], t_out_send),
        (out, out_recv),
    )
    for ref, sem in sent:
        pltpu.make_async_copy(ref, ref, sem).wait()


def shards(queries, keys, values, spatial_mask, temporal_mask):
    anywhere = pl.BlockSpec(memory_space=pl.ANY)
    held = pl.BlockSpec(memory_space=pltpu.HBM)
    dma = pltpu.SemaphoreType.DMA
    flops = 4 * HD * (ITEMS_S * SEQ_S**2 + ITEMS_T * SEQ_T**2)
    return pl.pallas_call(
        kernel,
        out_shape=pltpu.VMEM(queries.shape, queries.dtype),
        in_specs=[held] * 5,
        out_specs=anywhere,
        scratch_shapes=[
            pltpu.VMEM((ITEMS_S, 3 * SEQ_S, HD), jnp.bfloat16),
            pltpu.VMEM((CHUNKS, 3 * NF * FD, GP, CW), jnp.bfloat16),
            pltpu.VMEM((ITEMS_S, SEQ_S, HD), jnp.bfloat16),
            pltpu.VMEM((CHUNKS, NF * FD, GP, CW), jnp.bfloat16),
            pltpu.VMEM((ITEMS_S, NB_S, NB_S, 32), jnp.int32),
            pltpu.VMEM((ITEMS_T, NB_T, NB_T, 64), jnp.int32),
            pltpu.VMEM((ITEMS_S * NB_S, NB_S, BLOCK), jnp.float32),
            pltpu.VMEM((ITEMS_T * NB_T, NB_T, BLOCK), jnp.float32),
            pltpu.VMEM((SEQ_S, TQ), jnp.float32),
            pltpu.VMEM((HD + 16, SEQ_S), jnp.bfloat16),
            dma((2,)),
            dma((STAGES,)),
            dma,
            dma,
            dma,
            dma,
            dma,
        ],
        compiler_params=pltpu.CompilerParams(
            collective_id=0, has_side_effects=True, vmem_limit_bytes=50 * 2**20
        ),
        cost_estimate=pl.CostEstimate(
            flops=flops, bytes_accessed=4 * queries.size * 2, transcendentals=flops // (4 * HD)
        ),
    )(
        queries,
        keys,
        values,
        spatial_mask.transpose(1, 2, 3, 0),
        temporal_mask.transpose(1, 2, 3, 0),
    )


def solution(mesh):
    in_specs = (
        P("frame", "patch", None),
        P("frame", "patch", None),
        P("frame", "patch", None),
        P(),
        P(),
    )
    out_specs = P("frame", "patch", None)
    return jax.shard_map(shards, mesh=mesh, in_specs=in_specs, out_specs=out_specs, check_vma=False)
```

```python
import functools
import math

import jax
import jax.numpy as jnp
from jax import lax
from jax.experimental import pallas as pl
from jax.experimental.pallas import tpu as pltpu
from jax.sharding import PartitionSpec as P

HD = 128
SH = 28
TH = 12
GP = 32
BLOCK = 128
NF = 16
NP = 8
FD = 2
CELLS = 256
SEQ_S = NP * CELLS
SEQ_T = NF * FD * GP
NB_S = SEQ_S // BLOCK
NB_T = SEQ_T // BLOCK
ITEMS_S = FD * SH // NP
ITEMS_T = (CELLS // GP) * TH // NF
CHUNK = 2
CHUNKS = ITEMS_T // CHUNK
CW = CHUNK * HD
STAGES = ITEMS_S + CHUNKS
HOLD = 7
AHEAD = 5
TQ = 256
KC = 256
UNITS = 1.0 / math.sqrt(HD) * math.log2(math.e)
BIG = 1e30
MESH = pl.DeviceIdType.MESH


def attend(get_query, get_key, get_value, get_mask, put, first, order, length, scores_ref, value_ref):
    tiles = length // TQ
    halves = TQ // BLOCK
    for c in range(length // KC):
        value_ref[0:HD, c * KC : (c + 1) * KC] = get_value(c * KC, KC).T

    def step(d):
        tile = lax.rem(first + order(d), tiles)
        start = pl.multiple_of(tile * TQ, TQ)
        scaled = get_query(start, TQ).astype(jnp.float32) * UNITS
        high = scaled.astype(jnp.bfloat16)
        low = (scaled - high.astype(jnp.float32)).astype(jnp.bfloat16)
        query = jnp.concatenate([high, low], axis=1)

        def choose(j, rows, otherwise):
            parts = [
                jnp.where(
                    get_mask(tile * halves + i, j) > 0,
                    rows[:, i * BLOCK : (i + 1) * BLOCK],
                    otherwise,
                )
                for i in range(halves)
            ]
            return jnp.concatenate(parts, axis=1)

        top = jnp.full((8, TQ), -BIG, jnp.float32)
        for c in range(length // KC):
            key = get_key(c * KC, KC)
            scores = lax.dot_general(
                jnp.concatenate([key, key], axis=1),
                query,
                (((1,), (1,)), ((), ())),
                preferred_element_type=jnp.float32,
            )
            scores_ref[c * KC : (c + 1) * KC, :] = scores
            for b in range(KC // BLOCK):
                most = jnp.max(scores[b * BLOCK : (b + 1) * BLOCK].reshape(-1, 8, TQ), axis=0)
                top = jnp.maximum(top, choose(c * (KC // BLOCK) + b, most, -BIG))
        top = jnp.max(top, axis=0, keepdims=True)
        mixed = jnp.zeros((HD + 16, TQ), jnp.float32)
        for c in range(length // KC):
            parts = []
            for b in range(KC // BLOCK):
                j = c * (KC // BLOCK) + b
                shift = choose(j, top, BIG)
                parts.append(
                    jnp.exp2(scores_ref[j * BLOCK : (j + 1) * BLOCK, :] - shift).astype(jnp.bfloat16)
                )
            mixed = mixed + jnp.dot(
                value_ref[:, c * KC : (c + 1) * KC],
                jnp.concatenate(parts, axis=0),
                preferred_element_type=jnp.float32,
            )
        result = mixed[0:HD] * (1.0 / mixed[HD : HD + 1])
        put(tile, start, result.T.astype(jnp.bfloat16))

    pl.loop(0, tiles)(step)


def kernel(
    queries,
    keys,
    values,
    spatial_mask,
    temporal_mask,
    out,
    s_in,
    t_in,
    s_out,
    t_out,
    s_mask_in,
    t_mask_in,
    s_mask,
    t_mask,
    scores_ref,
    value_ref,
    mask_sem,
    in_recv,
    s_send,
    t_send,
    s_out_send,
    t_out_send,
    out_recv,
):
    me_f = lax.axis_index("frame")
    me_p = lax.axis_index("patch")
    tensors = (queries, keys, values)

    mask_copies = (
        pltpu.make_async_copy(
            spatial_mask.at[pl.ds(lax.rem(me_p, 4) * ITEMS_S, ITEMS_S)], s_mask_in, mask_sem.at[0]
        ),
        pltpu.make_async_copy(
            temporal_mask.at[pl.ds(lax.rem(me_f, 2) * ITEMS_T, ITEMS_T)], t_mask_in, mask_sem.at[1]
        ),
    )
    for copy in mask_copies:
        copy.start()

    barrier = pltpu.get_barrier_semaphore()

    @pl.loop(1, NP)
    def _(d):
        pl.semaphore_signal(
            barrier, inc=1, device_id=(me_f, lax.rem(me_p + d, NP)), device_id_type=MESH
        )

    @pl.loop(1, NF)
    def _(d):
        pl.semaphore_signal(
            barrier, inc=1, device_id=(lax.rem(me_f + d, NF), me_p), device_id_type=MESH
        )

    pl.semaphore_wait(barrier, NP + NF - 2)

    def spatial_place(rank, n):
        item = rank * ITEMS_S + n
        frame = item // SH
        return frame, pl.multiple_of((item - frame * SH) * HD, HD)

    def temporal_place(rank, c):
        group = rank // 2
        head = SH + (rank - group * 2) * ITEMS_T + c * CHUNK
        return pl.multiple_of(group * GP, GP), pl.multiple_of(head * HD, HD)

    def is_temporal(s):
        return lax.rem(s, 4) == 1

    def spatial_index(s):
        return s - (s + 2) // 4

    def start_spatial(s):
        n = spatial_index(s)

        def parts(rank):
            frame, column = spatial_place(rank, n)
            for i, tensor in enumerate(tensors):
                yield (
                    tensor.at[frame, :, pl.ds(column, HD)],
                    s_in.at[n, pl.ds(pl.multiple_of(i * SEQ_S + me_p * CELLS, CELLS), CELLS)],
                )

        @pl.loop(1, NP)
        def _(d):
            rank = lax.rem(me_p + d, NP)
            for source, target in parts(rank):
                pltpu.make_async_remote_copy(
                    src_ref=source,
                    dst_ref=target,
                    send_sem=s_send,
                    recv_sem=in_recv.at[s],
                    device_id=(me_f, rank),
                    device_id_type=MESH,
                ).start()

        for source, target in parts(me_p):
            pltpu.make_async_copy(source, target, in_recv.at[s]).start()

    def start_temporal(s):
        c = s // 4

        def parts(rank):
            row, column = temporal_place(rank, c)
            for i, tensor in enumerate(tensors):
                yield (
                    tensor.at[:, pl.ds(row, GP), pl.ds(column, CW)],
                    t_in.at[c, pl.ds(i * NF * FD + me_f * FD, FD)],
                )

        @pl.loop(1, NF)
        def _(d):
            rank = lax.rem(me_f + d, NF)
            for source, target in parts(rank):
                pltpu.make_async_remote_copy(
                    src_ref=source,
                    dst_ref=target,
                    send_sem=t_send,
                    recv_sem=in_recv.at[s],
                    device_id=(rank, me_p),
                    device_id_type=MESH,
                ).start()

        for source, target in parts(me_f):
            pltpu.make_async_copy(source, target, in_recv.at[s]).start()

    def start_stage(s):
        @pl.when(is_temporal(s))
        def _():
            start_temporal(s)

        @pl.when(jnp.logical_not(is_temporal(s)))
        def _():
            start_spatial(s)

    pl.loop(0, AHEAD)(start_stage)

    for copy in mask_copies:
        copy.wait()
    s_lane = me_f * FD + me_p // 4
    t_lane = me_p * (CELLS // GP) + me_f // 2

    def spread(rows, lane):
        lanes = lax.broadcasted_iota(jnp.int32, rows.shape, 2)
        chosen = jnp.sum(jnp.where(lanes == lane, rows.astype(jnp.float32), 0.0), axis=2, keepdims=True)
        return jnp.broadcast_to(chosen, rows.shape[:2] + (BLOCK,))

    @pl.loop(0, ITEMS_S)
    def _(n):
        s_mask[pl.ds(n * NB_S, NB_S)] = spread(s_mask_in[n], s_lane)

    @pl.loop(0, ITEMS_T)
    def _(n):
        t_mask[pl.ds(n * NB_T, NB_T)] = spread(t_mask_in[n], t_lane)

    value_ref[HD:, :] = jnp.ones((16, SEQ_S), jnp.bfloat16)

    beside = me_p + 1 - 2 * lax.rem(me_p, 2)

    def spatial_rows(n, rank):
        frame, column = spatial_place(me_p, n)
        return (
            s_out.at[n, pl.ds(pl.multiple_of(rank * CELLS, CELLS), CELLS)],
            out.at[frame, :, pl.ds(column, HD)],
        )

    def give_spatial(n, rank):
        source, target = spatial_rows(n, rank)
        pltpu.make_async_remote_copy(
            src_ref=source,
            dst_ref=target,
            send_sem=s_out_send,
            recv_sem=out_recv,
            device_id=(me_f, rank),
            device_id_type=MESH,
        ).start()

    def work_spatial(s):
        n = spatial_index(s)
        pltpu.make_async_copy(s_in.at[n], s_in.at[n], in_recv.at[s]).wait()

        def put(tile, start, rows):
            s_out[n, pl.ds(start, TQ), :] = rows
            held = (tile == beside) & (n >= ITEMS_S - HOLD)

            @pl.when((tile != me_p) & jnp.logical_not(held))
            def _():
                give_spatial(n, tile)

            @pl.when(tile == me_p)
            def _():
                source, target = spatial_rows(n, tile)
                pltpu.make_async_copy(source, target, out_recv).start()

        attend(
            lambda a, l: s_in[n, pl.ds(a, l), :],
            lambda a, l: s_in[n, pl.ds(SEQ_S + a, l), :],
            lambda a, l: s_in[n, pl.ds(2 * SEQ_S + a, l), :],
            lambda i, j: s_mask[n * NB_S + i, j : j + 1, :],
            put,
            me_p + 1,
            lambda d: d,
            SEQ_S,
            scores_ref,
            value_ref,
        )

    def work_temporal(s):
        c = s // 4
        pltpu.make_async_copy(t_in.at[c], t_in.at[c], in_recv.at[s]).wait()
        row, column = temporal_place(me_f, c)
        ranks = TQ // (FD * GP)

        @pl.loop(0, CHUNK)
        def _(h):
            lanes = pl.ds(pl.multiple_of(h * HD, HD), HD)

            def get(i):
                def rows(a, l):
                    return t_in[c, pl.ds(i * NF * FD + a // GP, l // GP), :, lanes].reshape(l, HD)

                return rows

            def put(tile, start, rows):
                frame = tile * (TQ // GP)
                t_out[c, pl.ds(frame, TQ // GP), :, lanes] = rows.reshape(TQ // GP, GP, HD)
                target = out.at[
                    :, pl.ds(row, GP), pl.ds(pl.multiple_of(column + h * HD, HD), HD)
                ]

                for e in range(ranks):
                    rank = tile * ranks + e
                    source = t_out.at[c, pl.ds(rank * FD, FD), :, lanes]

                    @pl.when(rank != me_f)
                    def _():
                        pltpu.make_async_remote_copy(
                            src_ref=source,
                            dst_ref=target,
                            send_sem=t_out_send,
                            recv_sem=out_recv,
                            device_id=(rank, me_p),
                            device_id_type=MESH,
                        ).start()

                    @pl.when(rank == me_f)
                    def _():
                        pltpu.make_async_copy(source, target, out_recv).start()

            item = (c * CHUNK + h) * NB_T
            attend(
                get(0),
                get(1),
                get(2),
                lambda i, j: t_mask[item + i, j : j + 1, :],
                put,
                me_f // ranks + 1,
                lambda d: jnp.where(d < 2, 1 - d, d),
                SEQ_T,
                scores_ref,
                value_ref,
            )

    @pl.loop(0, STAGES)
    def _(s):
        @pl.when(s + AHEAD < STAGES)
        def _():
            start_stage(s + AHEAD)

        @pl.when(is_temporal(s))
        def _():
            work_temporal(s)

        @pl.when(jnp.logical_not(is_temporal(s)))
        def _():
            work_spatial(s)

    @pl.loop(ITEMS_S - HOLD, ITEMS_S)
    def _(n):
        give_spatial(n, beside)

    sent = (
        (s_in.at[:, pl.ds(0, 3 * (NP - 1) * CELLS)], s_send),
        (t_in.at[:, pl.ds(0, 3 * (NF - 1) * FD)], t_send),
        (s_out.at[:, pl.ds(0, (NP - 1) * CELLS)], s_out_send),
        (t_out.at[:, pl.ds(0, (NF - 1) * FD)], t_out_send),
        (out, out_recv),
    )
    for ref, sem in sent:
        pltpu.make_async_copy(ref, ref, sem).wait()


def shards(queries, keys, values, spatial_mask, temporal_mask):
    anywhere = pl.BlockSpec(memory_space=pl.ANY)
    held = pl.BlockSpec(memory_space=pltpu.HBM)
    dma = pltpu.SemaphoreType.DMA
    flops = 4 * HD * (ITEMS_S * SEQ_S**2 + ITEMS_T * SEQ_T**2)
    return pl.pallas_call(
        kernel,
        out_shape=pltpu.VMEM(queries.shape, queries.dtype),
        in_specs=[held] * 5,
        out_specs=anywhere,
        scratch_shapes=[
            pltpu.VMEM((ITEMS_S, 3 * SEQ_S, HD), jnp.bfloat16),
            pltpu.VMEM((CHUNKS, 3 * NF * FD, GP, CW), jnp.bfloat16),
            pltpu.VMEM((ITEMS_S, SEQ_S, HD), jnp.bfloat16),
            pltpu.VMEM((CHUNKS, NF * FD, GP, CW), jnp.bfloat16),
            pltpu.VMEM((ITEMS_S, NB_S, NB_S, 32), jnp.int32),
            pltpu.VMEM((ITEMS_T, NB_T, NB_T, 64), jnp.int32),
            pltpu.VMEM((ITEMS_S * NB_S, NB_S, BLOCK), jnp.float32),
            pltpu.VMEM((ITEMS_T * NB_T, NB_T, BLOCK), jnp.float32),
            pltpu.VMEM((SEQ_S, TQ), jnp.float32),
            pltpu.VMEM((HD + 16, SEQ_S), jnp.bfloat16),
            dma((2,)),
            dma((STAGES,)),
            dma,
            dma,
            dma,
            dma,
            dma,
        ],
        compiler_params=pltpu.CompilerParams(
            collective_id=0, has_side_effects=True, vmem_limit_bytes=50 * 2**20
        ),
        cost_estimate=pl.CostEstimate(
            flops=flops, bytes_accessed=4 * queries.size * 2, transcendentals=flops // (4 * HD)
        ),
    )(
        queries,
        keys,
        values,
        spatial_mask.transpose(1, 2, 3, 0),
        temporal_mask.transpose(1, 2, 3, 0),
    )


def solution(mesh):
    in_specs = (
        P("frame", "patch", None),
        P("frame", "patch", None),
        P("frame", "patch", None),
        P(),
        P(),
    )
    out_specs = P("frame", "patch", None)
    return jax.shard_map(shards, mesh=mesh, in_specs=in_specs, out_specs=out_specs, check_vma=False)
```

```python
import functools
import math

import jax
import jax.numpy as jnp
from jax import lax
from jax.experimental import pallas as pl
from jax.experimental.pallas import tpu as pltpu
from jax.sharding import PartitionSpec as P

HD = 128
SH = 28
TH = 12
GP = 32
BLOCK = 128
NF = 16
NP = 8
FD = 2
CELLS = 256
SEQ_S = NP * CELLS
SEQ_T = NF * FD * GP
NB_S = SEQ_S // BLOCK
NB_T = SEQ_T // BLOCK
ITEMS_S = FD * SH // NP
ITEMS_T = (CELLS // GP) * TH // NF
CHUNK = 2
CHUNKS = ITEMS_T // CHUNK
CW = CHUNK * HD
STAGES = ITEMS_S + CHUNKS
HOLD = 4
AHEAD = 5
TQ = 256
KC = 256
UNITS = 1.0 / math.sqrt(HD) * math.log2(math.e)
BIG = 1e30
MESH = pl.DeviceIdType.MESH


def attend(get_query, get_key, get_value, get_mask, put, first, length, scores_ref, value_ref):
    tiles = length // TQ
    halves = TQ // BLOCK
    for c in range(length // KC):
        value_ref[0:HD, c * KC : (c + 1) * KC] = get_value(c * KC, KC).T

    def step(d):
        tile = lax.rem(first + d, tiles)
        start = pl.multiple_of(tile * TQ, TQ)
        scaled = get_query(start, TQ).astype(jnp.float32) * UNITS
        high = scaled.astype(jnp.bfloat16)
        low = (scaled - high.astype(jnp.float32)).astype(jnp.bfloat16)
        query = jnp.concatenate([high, low], axis=1)

        def choose(j, rows, otherwise):
            parts = [
                jnp.where(
                    get_mask(tile * halves + i, j) > 0,
                    rows[:, i * BLOCK : (i + 1) * BLOCK],
                    otherwise,
                )
                for i in range(halves)
            ]
            return jnp.concatenate(parts, axis=1)

        top = jnp.full((8, TQ), -BIG, jnp.float32)
        for c in range(length // KC):
            key = get_key(c * KC, KC)
            scores = lax.dot_general(
                jnp.concatenate([key, key], axis=1),
                query,
                (((1,), (1,)), ((), ())),
                preferred_element_type=jnp.float32,
            )
            scores_ref[c * KC : (c + 1) * KC, :] = scores
            for b in range(KC // BLOCK):
                most = jnp.max(scores[b * BLOCK : (b + 1) * BLOCK].reshape(-1, 8, TQ), axis=0)
                top = jnp.maximum(top, choose(c * (KC // BLOCK) + b, most, -BIG))
        top = jnp.max(top, axis=0, keepdims=True)
        mixed = jnp.zeros((HD + 16, TQ), jnp.float32)
        for c in range(length // KC):
            parts = []
            for b in range(KC // BLOCK):
                j = c * (KC // BLOCK) + b
                shift = choose(j, top, BIG)
                parts.append(
                    jnp.exp2(scores_ref[j * BLOCK : (j + 1) * BLOCK, :] - shift).astype(jnp.bfloat16)
                )
            mixed = mixed + jnp.dot(
                value_ref[:, c * KC : (c + 1) * KC],
                jnp.concatenate(parts, axis=0),
                preferred_element_type=jnp.float32,
            )
        result = mixed[0:HD] * (1.0 / mixed[HD : HD + 1])
        put(tile, start, result.T.astype(jnp.bfloat16))

    pl.loop(0, tiles)(step)


def kernel(
    queries,
    keys,
    values,
    spatial_mask,
    temporal_mask,
    out,
    s_in,
    t_in,
    s_out,
    t_out,
    s_mask_in,
    t_mask_in,
    s_mask,
    t_mask,
    scores_ref,
    value_ref,
    mask_sem,
    in_recv,
    s_send,
    t_send,
    s_out_send,
    t_out_send,
    out_recv,
):
    me_f = lax.axis_index("frame")
    me_p = lax.axis_index("patch")
    tensors = (queries, keys, values)

    barrier = pltpu.get_barrier_semaphore()

    @pl.loop(0, NF - 1)
    def _(k):
        d = jnp.where(k < NF // 2, k + NF // 2, k + 1 - NF // 2)
        pl.semaphore_signal(
            barrier, inc=1, device_id=(lax.rem(me_f + d, NF), me_p), device_id_type=MESH
        )

    @pl.loop(1, NP)
    def _(d):
        pl.semaphore_signal(
            barrier, inc=1, device_id=(me_f, lax.rem(me_p + d, NP)), device_id_type=MESH
        )

    mask_copies = (
        pltpu.make_async_copy(
            spatial_mask.at[pl.ds(lax.rem(me_p, 4) * ITEMS_S, ITEMS_S)], s_mask_in, mask_sem.at[0]
        ),
        pltpu.make_async_copy(
            temporal_mask.at[pl.ds(lax.rem(me_f, 2) * ITEMS_T, ITEMS_T)], t_mask_in, mask_sem.at[1]
        ),
    )
    for copy in mask_copies:
        copy.start()

    pl.semaphore_wait(barrier, NP + NF - 2)

    def spatial_place(rank, n):
        item = rank * ITEMS_S + n
        frame = item // SH
        return frame, pl.multiple_of((item - frame * SH) * HD, HD)

    def temporal_place(rank, c):
        group = rank // 2
        head = SH + (rank - group * 2) * ITEMS_T + c * CHUNK
        return pl.multiple_of(group * GP, GP), pl.multiple_of(head * HD, HD)

    def is_temporal(s):
        return lax.rem(s, 4) == 1

    def spatial_index(s):
        return s - (s + 2) // 4

    def start_spatial(s):
        n = spatial_index(s)

        def parts(rank):
            frame, column = spatial_place(rank, n)
            for i, tensor in enumerate(tensors):
                yield (
                    tensor.at[frame, :, pl.ds(column, HD)],
                    s_in.at[n, pl.ds(pl.multiple_of(i * SEQ_S + me_p * CELLS, CELLS), CELLS)],
                )

        @pl.loop(1, NP)
        def _(d):
            rank = lax.rem(me_p + d, NP)
            for source, target in parts(rank):
                pltpu.make_async_remote_copy(
                    src_ref=source,
                    dst_ref=target,
                    send_sem=s_send,
                    recv_sem=in_recv.at[s],
                    device_id=(me_f, rank),
                    device_id_type=MESH,
                ).start()

        for source, target in parts(me_p):
            pltpu.make_async_copy(source, target, in_recv.at[s]).start()

    def start_temporal(s):
        c = s // 4

        def parts(rank):
            row, column = temporal_place(rank, c)
            for i, tensor in enumerate(tensors):
                yield (
                    tensor.at[:, pl.ds(row, GP), pl.ds(column, CW)],
                    t_in.at[c, pl.ds(i * NF * FD + me_f * FD, FD)],
                )

        @pl.loop(1, NF)
        def _(d):
            rank = lax.rem(me_f + d, NF)
            for source, target in parts(rank):
                pltpu.make_async_remote_copy(
                    src_ref=source,
                    dst_ref=target,
                    send_sem=t_send,
                    recv_sem=in_recv.at[s],
                    device_id=(rank, me_p),
                    device_id_type=MESH,
                ).start()

        for source, target in parts(me_f):
            pltpu.make_async_copy(source, target, in_recv.at[s]).start()

    def start_stage(s):
        @pl.when(is_temporal(s))
        def _():
            start_temporal(s)

        @pl.when(jnp.logical_not(is_temporal(s)))
        def _():
            start_spatial(s)

    pl.loop(0, AHEAD)(start_stage)

    for copy in mask_copies:
        copy.wait()
    s_lane = me_f * FD + me_p // 4
    t_lane = me_p * (CELLS // GP) + me_f // 2

    def spread(rows, lane):
        lanes = lax.broadcasted_iota(jnp.int32, rows.shape, 2)
        chosen = jnp.sum(jnp.where(lanes == lane, rows.astype(jnp.float32), 0.0), axis=2, keepdims=True)
        return jnp.broadcast_to(chosen, rows.shape[:2] + (BLOCK,))

    @pl.loop(0, ITEMS_S)
    def _(n):
        s_mask[pl.ds(n * NB_S, NB_S)] = spread(s_mask_in[n], s_lane)

    @pl.loop(0, ITEMS_T)
    def _(n):
        t_mask[pl.ds(n * NB_T, NB_T)] = spread(t_mask_in[n], t_lane)

    value_ref[HD:, :] = jnp.ones((16, SEQ_S), jnp.bfloat16)

    beside = me_p + 1 - 2 * lax.rem(me_p, 2)

    def spatial_rows(n, rank):
        frame, column = spatial_place(me_p, n)
        return (
            s_out.at[n, pl.ds(pl.multiple_of(rank * CELLS, CELLS), CELLS)],
            out.at[frame, :, pl.ds(column, HD)],
        )

    def give_spatial(n, rank):
        source, target = spatial_rows(n, rank)
        pltpu.make_async_remote_copy(
            src_ref=source,
            dst_ref=target,
            send_sem=s_out_send,
            recv_sem=out_recv,
            device_id=(me_f, rank),
            device_id_type=MESH,
        ).start()

    def work_spatial(s):
        n = spatial_index(s)
        pltpu.make_async_copy(s_in.at[n], s_in.at[n], in_recv.at[s]).wait()

        def put(tile, start, rows):
            s_out[n, pl.ds(start, TQ), :] = rows
            held = (tile == beside) & (n >= ITEMS_S - HOLD)

            @pl.when((tile != me_p) & jnp.logical_not(held))
            def _():
                give_spatial(n, tile)

            @pl.when(tile == me_p)
            def _():
                source, target = spatial_rows(n, tile)
                pltpu.make_async_copy(source, target, out_recv).start()

        attend(
            lambda a, l: s_in[n, pl.ds(a, l), :],
            lambda a, l: s_in[n, pl.ds(SEQ_S + a, l), :],
            lambda a, l: s_in[n, pl.ds(2 * SEQ_S + a, l), :],
            lambda i, j: s_mask[n * NB_S + i, j : j + 1, :],
            put,
            me_p + 1,
            SEQ_S,
            scores_ref,
            value_ref,
        )

    def work_temporal(s):
        c = s // 4
        pltpu.make_async_copy(t_in.at[c], t_in.at[c], in_recv.at[s]).wait()
        row, column = temporal_place(me_f, c)
        ranks = TQ // (FD * GP)

        @pl.loop(0, CHUNK)
        def _(h):
            lanes = pl.ds(pl.multiple_of(h * HD, HD), HD)

            def get(i):
                def rows(a, l):
                    return t_in[c, pl.ds(i * NF * FD + a // GP, l // GP), :, lanes].reshape(l, HD)

                return rows

            def put(tile, start, rows):
                frame = tile * (TQ // GP)
                t_out[c, pl.ds(frame, TQ // GP), :, lanes] = rows.reshape(TQ // GP, GP, HD)
                target = out.at[
                    :, pl.ds(row, GP), pl.ds(pl.multiple_of(column + h * HD, HD), HD)
                ]

                for e in range(ranks):
                    rank = tile * ranks + e
                    source = t_out.at[c, pl.ds(rank * FD, FD), :, lanes]

                    @pl.when(rank != me_f)
                    def _():
                        pltpu.make_async_remote_copy(
                            src_ref=source,
                            dst_ref=target,
                            send_sem=t_out_send,
                            recv_sem=out_recv,
                            device_id=(rank, me_p),
                            device_id_type=MESH,
                        ).start()

                    @pl.when(rank == me_f)
                    def _():
                        pltpu.make_async_copy(source, target, out_recv).start()

            item = (c * CHUNK + h) * NB_T
            attend(
                get(0),
                get(1),
                get(2),
                lambda i, j: t_mask[item + i, j : j + 1, :],
                put,
                me_f // ranks + 1,
                SEQ_T,
                scores_ref,
                value_ref,
            )

    @pl.loop(0, STAGES)
    def _(s):
        @pl.when(s + AHEAD < STAGES)
        def _():
            start_stage(s + AHEAD)

        @pl.when(is_temporal(s))
        def _():
            work_temporal(s)

        @pl.when(jnp.logical_not(is_temporal(s)))
        def _():
            work_spatial(s)

    @pl.loop(ITEMS_S - HOLD, ITEMS_S)
    def _(n):
        give_spatial(n, beside)

    sent = (
        (s_in.at[:, pl.ds(0, 3 * (NP - 1) * CELLS)], s_send),
        (t_in.at[:, pl.ds(0, 3 * (NF - 1) * FD)], t_send),
        (s_out.at[:, pl.ds(0, (NP - 1) * CELLS)], s_out_send),
        (t_out.at[:, pl.ds(0, (NF - 1) * FD)], t_out_send),
        (out, out_recv),
    )
    for ref, sem in sent:
        pltpu.make_async_copy(ref, ref, sem).wait()


def shards(queries, keys, values, spatial_mask, temporal_mask):
    anywhere = pl.BlockSpec(memory_space=pl.ANY)
    held = pl.BlockSpec(memory_space=pltpu.HBM)
    dma = pltpu.SemaphoreType.DMA
    flops = 4 * HD * (ITEMS_S * SEQ_S**2 + ITEMS_T * SEQ_T**2)
    return pl.pallas_call(
        kernel,
        out_shape=pltpu.VMEM(queries.shape, queries.dtype),
        in_specs=[held] * 5,
        out_specs=anywhere,
        scratch_shapes=[
            pltpu.VMEM((ITEMS_S, 3 * SEQ_S, HD), jnp.bfloat16),
            pltpu.VMEM((CHUNKS, 3 * NF * FD, GP, CW), jnp.bfloat16),
            pltpu.VMEM((ITEMS_S, SEQ_S, HD), jnp.bfloat16),
            pltpu.VMEM((CHUNKS, NF * FD, GP, CW), jnp.bfloat16),
            pltpu.VMEM((ITEMS_S, NB_S, NB_S, 32), jnp.int32),
            pltpu.VMEM((ITEMS_T, NB_T, NB_T, 64), jnp.int32),
            pltpu.VMEM((ITEMS_S * NB_S, NB_S, BLOCK), jnp.float32),
            pltpu.VMEM((ITEMS_T * NB_T, NB_T, BLOCK), jnp.float32),
            pltpu.VMEM((SEQ_S, TQ), jnp.float32),
            pltpu.VMEM((HD + 16, SEQ_S), jnp.bfloat16),
            dma((2,)),
            dma((STAGES,)),
            dma,
            dma,
            dma,
            dma,
            dma,
        ],
        compiler_params=pltpu.CompilerParams(
            collective_id=0, has_side_effects=True, vmem_limit_bytes=50 * 2**20
        ),
        cost_estimate=pl.CostEstimate(
            flops=flops, bytes_accessed=4 * queries.size * 2, transcendentals=flops // (4 * HD)
        ),
    )(
        queries,
        keys,
        values,
        spatial_mask.transpose(1, 2, 3, 0),
        temporal_mask.transpose(1, 2, 3, 0),
    )


def solution(mesh):
    in_specs = (
        P("frame", "patch", None),
        P("frame", "patch", None),
        P("frame", "patch", None),
        P(),
        P(),
    )
    out_specs = P("frame", "patch", None)
    return jax.shard_map(shards, mesh=mesh, in_specs=in_specs, out_specs=out_specs, check_vma=False)
```
